256 devices in a mesh: rep: 8 (over y_lo, x), fsdp: 32 (over z, y_hi, core).
Axes of the slice: x: 4, y: 4 (y_hi: 2, y_lo: 2; y = y_hi * 2 + y_lo), z: 8, core: 2. Of those that a mesh axis runs over, the one named last changes fastest.
Arguments:
- hidden_states: bfloat16 [65536, 8192], P(('rep', 'fsdp')), may hold values from -6 to 6
- queries: bfloat16 [65536, 4096], P(('rep', 'fsdp')), may hold values from -170 to 170
- token_ids: int32 [65536], P(('rep', 'fsdp')), may hold values from 0 to 128000, as said below
- local_weights: bfloat16 [8, 8192, 1024], P('rep', 'fsdp'), may hold values from -0.0625 to 0.0625
- outer_base: float32 [8192, 1024], P('fsdp'), may hold values from -1 to 1
- momentum: float32 [8192, 1024], P('fsdp'), may hold values from -0.08 to 0.08
- outer_rates: float32 [8], replicated, may hold values from 0.2 to 1
- frag_index: int32 [1], replicated, may hold values from 0 to 7
Outputs:
- context: bfloat16 [65536, 4096], P(('rep', 'fsdp'))
- new_base: float32 [8192, 1024], P('fsdp')
- new_momentum: float32 [8192, 1024], P('fsdp')
The draws below stay inside these ranges and needn't reach their ends.
Inputs may be any that keep to these rules, and one draw needn't show every extreme that they name: `token_ids`: each device's first token, at a multiple of 256, has id 128000; ids below 128000 are ordinary tokens.
All inputs are finite; a program needn't handle non-finite values.
Results may differ from the reference program's by a relative error of at most 0.006.
Values may be sent and summed in bfloat16 or wider, within the bound.
No kernel may reach another device: no remote copies, remote signals or barrier semaphores. Data moves between devices by JAX's collectives and lax.ppermute only.
A program may use at most 128 MiB of HBM per device.

```python
import math
import jax
import jax.numpy as jnp
import numpy as np
from jax import lax

D = 8192
HEAD = 128
BLOCK = 32
FRAGS = 8
BOS = 128000
TOK_DEV = 256
QH = 32
KV_COLS = 1024
TOKENS = 65536
N_REP = 8


def draw_token_ids(key, part):
    key = jax.random.fold_in(key, 11)
    first_key, second_key = jax.random.split(key)
    drawn_ids = jax.random.randint(first_key, (TOKENS,), 0, BOS, dtype=jnp.int32)
    mark_draws = jax.random.randint(second_key, (TOKENS,), 0, max(TOK_DEV // 4, 2), dtype=jnp.int32)
    position_idx = jnp.arange(TOKENS, dtype=jnp.int32)
    starts = (mark_draws == 0) | (position_idx % TOK_DEV == 0)
    marked = jnp.where(starts, BOS, drawn_ids)
    return jnp.where(position_idx == 1, 0, marked).astype(jnp.int32)


def draw_queries(key, part):
    key = jax.random.fold_in(key, 23)
    first_key = jax.random.fold_in(key, 0)
    entries = jax.random.normal(first_key, (TOKENS, QH * HEAD), jnp.float32)
    return jnp.clip(entries, -6.0, 6.0).astype(jnp.bfloat16)


def draw_outer_base(key, part):
    key = jax.random.fold_in(key, 37)
    entries = jnp.clip(jax.random.normal(key, (D, KV_COLS), jnp.float32), -6.0, 6.0)
    narrowed = lax.optimization_barrier((entries * (1.0 / math.sqrt(D))).astype(jnp.bfloat16))
    return narrowed.astype(jnp.float32)


def levels(own_key, dims, cuts, smallest, high):
    factor_of, own = 1.0, jax.random.fold_in(own_key, 6)
    for axis_at, blocks in cuts:
        heights = jnp.exp(jax.random.uniform(jax.random.fold_in(own, axis_at), (blocks,), jnp.float32, smallest / len(cuts), high / len(cuts)))
        factor_of = factor_of * jnp.repeat(heights, dims[axis_at] // blocks).reshape([-1 if axis == axis_at else 1 for axis in range(len(dims))])
    return factor_of


def centred(own_key, dims, scale, bound, cuts=(), kind=jnp.bfloat16):
    array = scale * jax.random.normal(own_key, dims, jnp.float32)
    if cuts:
        array = array * levels(own_key, dims, cuts, -0.22, 0.18)
    return jnp.clip(array, -bound, bound).astype(kind)


def setup_inputs(seed: int = 0) -> dict:
    arg_keys = jax.random.split(jax.random.key(seed), 9)
    hidden_states = centred(arg_keys[0], (TOKENS, D), 1.0, 6.0, ((0, 256),))
    queries = draw_queries(jax.random.fold_in(arg_keys[8], 71), 0)
    token_ids = draw_token_ids(jax.random.fold_in(arg_keys[8], 71), 0)
    local_weights = centred(arg_keys[3], (N_REP, D, KV_COLS), D ** -0.5, 0.0625, ((0, 8), (1, 32)))
    outer_base = draw_outer_base(jax.random.fold_in(arg_keys[8], 71), 0)
    momentum = centred(arg_keys[5], (D, KV_COLS), 0.01, 0.08, ((0, 32),), jnp.float32)
    outer_rates = jnp.clip(jnp.exp(jax.random.uniform(arg_keys[6], (FRAGS,), jnp.float32, math.log(0.2), math.log(1.0))), 0.2, 1.0)
    frag_index = jax.random.randint(arg_keys[7], (1,), 0, FRAGS).astype(jnp.int32)
    return {"hidden_states": hidden_states, "queries": queries, "token_ids": token_ids, "local_weights": local_weights, "outer_base": outer_base, "momentum": momentum, "outer_rates": outer_rates, "frag_index": frag_index}


rope_base = 500000.0
momentum_coef = 0.9

def rotate(head_vals, positions):
    half_dim = head_vals.shape[-1] // 2
    steps_idx = jnp.arange(half_dim, dtype=jnp.float32)
    inverse = rope_base ** (-2.0 * steps_idx / head_vals.shape[-1])
    angles = positions[:, None] * inverse[None, :]
    cosine = jnp.cos(angles)[:, None, :]
    sine_part = jnp.sin(angles)[:, None, :]
    first_half = head_vals[..., :half_dim]
    second_half = head_vals[..., half_dim:]
    return jnp.concatenate([first_half * cosine - second_half * sine_part, second_half * cosine + first_half * sine_part], axis=-1)

def layout(token_row):
    token_count = token_row.shape[0]
    starts = token_row == BOS
    position_idx = jnp.arange(token_count, dtype=jnp.int32)
    latest = lax.cummax(jnp.where(starts, position_idx, 0), axis=0)
    positions = (position_idx - latest).astype(jnp.float32)
    documents = jnp.cumsum(starts.astype(jnp.int32))
    allowed = (documents[:, None] == documents[None, :]) & (position_idx[None, :] <= position_idx[:, None])
    return (positions, allowed)

def attend(kv_rows, query_rows, token_row):
    positions, allowed = layout(token_row)
    token_count = query_rows.shape[0]
    kv_heads = kv_rows.shape[1] // (2 * HEAD)
    query_heads = query_rows.shape[1] // HEAD
    key_rows = rotate(kv_rows[:, :kv_heads * HEAD].reshape(token_count, kv_heads, HEAD), positions).astype(jnp.bfloat16)
    value_rows = kv_rows[:, kv_heads * HEAD:].reshape(token_count, kv_heads, HEAD).astype(jnp.bfloat16)
    rotated = rotate(query_rows.astype(jnp.float32).reshape(token_count, query_heads, HEAD), positions).astype(jnp.bfloat16)
    grouped = rotated.reshape(token_count, kv_heads, query_heads // kv_heads, HEAD)
    scores = jnp.einsum('tkgd,skd->kgts', grouped.astype(jnp.float32), key_rows.astype(jnp.float32)) / math.sqrt(HEAD)
    scores = jnp.where(allowed[None, None], scores, -1e+30)
    row_peak = lax.optimization_barrier(jnp.max(scores, axis=-1, keepdims=True))
    exponent = jnp.exp(scores - row_peak)
    weights = (exponent / lax.optimization_barrier(jnp.sum(exponent, axis=-1, keepdims=True))).astype(jnp.bfloat16)
    context = jnp.einsum('kgts,skd->tkgd', weights.astype(jnp.float32), value_rows.astype(jnp.float32))
    return context.reshape(token_count, query_heads * HEAD).astype(jnp.bfloat16)

def encode(delta):
    shard_rows = delta.shape[0]
    blocks = delta.reshape(shard_rows, delta.shape[1] // BLOCK, BLOCK)
    block_peak = lax.optimization_barrier(jnp.max(jnp.abs(blocks), axis=-1))
    block_exp = jnp.full(block_peak.shape, -30, jnp.int32)
    for level in range(-29, 3):
        block_exp = block_exp + (block_peak >= np.float32(2.0 ** level)).astype(jnp.int32)
    block_scale = jnp.zeros(block_peak.shape, jnp.float32)
    block_inverse = jnp.zeros(block_peak.shape, jnp.float32)
    for level in range(-30, 3):
        chosen = block_exp == level
        block_scale = jnp.where(chosen, np.float32(2.0 ** (level - 8)), block_scale)
        block_inverse = jnp.where(chosen, np.float32(2.0 ** (8 - level)), block_inverse)
    scaled = blocks * block_inverse[..., None]
    magnitude = jnp.abs(scaled)
    element_exp = jnp.full(magnitude.shape, -6, jnp.int32)
    for level in range(-5, 9):
        element_exp = element_exp + (magnitude >= np.float32(2.0 ** level)).astype(jnp.int32)
    step_size = jnp.zeros(magnitude.shape, jnp.float32)
    step_inverse = jnp.zeros(magnitude.shape, jnp.float32)
    for level in range(-6, 9):
        chosen = element_exp == level
        step_size = jnp.where(chosen, np.float32(2.0 ** (level - 3)), step_size)
        step_inverse = jnp.where(chosen, np.float32(2.0 ** (3 - level)), step_inverse)
    counted = jnp.floor(magnitude * step_inverse + 0.5)
    coded_vals = jnp.sign(scaled) * jnp.minimum(counted * step_size, 448.0)
    return (coded_vals.astype(jnp.bfloat16), block_scale.astype(jnp.bfloat16))

def reference(hidden_states, queries, token_ids, local_weights, outer_base, momentum, outer_rates, frag_index):
    groups = local_weights.shape[0]
    shards = hidden_states.shape[0] // (groups * TOK_DEV)
    states = hidden_states.reshape(groups, shards * TOK_DEV, D)
    query_blocks = queries.reshape(groups, shards, TOK_DEV, queries.shape[1])
    token_blocks = token_ids.reshape(groups, shards, TOK_DEV)

    def one_device(packed):
        return attend(packed[0], packed[1], packed[2])

    def one_group(packed):
        state_rows, query_rows, token_rows, weight_rows = packed
        kv_all = jnp.dot(state_rows, weight_rows, preferred_element_type=jnp.float32)
        kv_all = kv_all.reshape(shards, TOK_DEV, weight_rows.shape[1])
        return lax.map(one_device, (kv_all, query_rows, token_rows))
    context = lax.map(one_group, (states, query_blocks, token_blocks, local_weights))
    context = context.reshape(hidden_states.shape[0], queries.shape[1])

    def add_group(total, weight_rows):
        delta = outer_base - weight_rows.astype(jnp.float32)
        codes, scales = encode(delta)
        decoded = codes.astype(jnp.float32) * scales.astype(jnp.float32)[..., None]
        return (total + decoded.reshape(D, KV_COLS), None)
    total, _ = lax.scan(add_group, jnp.zeros((D, KV_COLS), jnp.float32), local_weights)
    outer_grad = total / groups
    rate = outer_rates[frag_index[0]]
    new_momentum = momentum_coef * momentum + outer_grad
    new_base = outer_base - rate * (outer_grad + momentum_coef * new_momentum)
    return (context, new_base, new_momentum)
```

```python
import functools
import math

import jax
import jax.numpy as jnp
from jax import lax
from jax.experimental import pallas as pl
from jax.experimental.pallas import tpu as pltpu
from jax.sharding import PartitionSpec as P

HEAD = 128
BLOCK = 32
BOS = 128000
TOK = 256
ROWS = 256
KV_HEADS = 4
HALF = KV_HEADS * HEAD
GROUP_HEADS = 8
Z, Y_HI, CORES = 8, 2, 2
X = 4

rope_base = 500000.0
momentum_coef = 0.9
F32 = jnp.float32
BF16 = jnp.bfloat16


def fsdp_pairs(move):
    pairs = []
    for z in range(Z):
        for y in range(Y_HI):
            for c in range(CORES):
                z2, y2, c2 = move(z, y, c)
                pairs.append(
                    (
                        (z * Y_HI + y) * CORES + c,
                        ((z2 % Z) * Y_HI + y2 % Y_HI) * CORES + c2 % CORES,
                    )
                )
    return pairs


UP = fsdp_pairs(lambda z, y, c: (z + 1, y, c))
DOWN = fsdp_pairs(lambda z, y, c: (z - 1, y, c))
ACROSS = fsdp_pairs(lambda z, y, c: (z, y + 1, c))
SWAP = fsdp_pairs(lambda z, y, c: (z, y, c + 1))


def send(block, pairs):
    return lax.ppermute(block, "fsdp", pairs)


def tie(*arrays):
    return lax.optimization_barrier(arrays)


def pick_kernel(core_ref, hidden_ref, out_ref):
    out_ref[...] = hidden_ref[...]


def pick_columns(hidden, core):
    blocks = Z * Y_HI
    return pl.pallas_call(
        pick_kernel,
        out_shape=jax.ShapeDtypeStruct((TOK, blocks * ROWS), BF16),
        grid_spec=pltpu.PrefetchScalarGridSpec(
            num_scalar_prefetch=1,
            grid=(blocks,),
            in_specs=[pl.BlockSpec((TOK, ROWS), lambda i, core: (0, 2 * i + 1 - core[0]))],
            out_specs=pl.BlockSpec((TOK, ROWS), lambda i, core: (0, i)),
        ),
        cost_estimate=pl.CostEstimate(
            flops=0, bytes_accessed=4 * TOK * blocks * ROWS, transcendentals=0
        ),
    )(core, hidden)


def multiply_kernel(n_h, uses, index_ref, *refs):
    own, other = refs[:n_h], refs[n_h : 2 * n_h]
    n_w = len(uses)
    weights = refs[2 * n_h : 2 * n_h + n_w]
    rest = refs[2 * n_h + n_w :]
    totals, outs = (rest[:4], rest[4:]) if len(rest) == 8 else (None, rest)
    for side in range(2):
        states = (own, other)[side]
        for part in range(2):
            total = None if totals is None else totals[2 * side + part][...]
            for (cols, where), weight in zip(uses, weights):
                if where != part:
                    continue
                left = [states[k][...] for k in cols]
                left = left[0] if len(left) == 1 else jnp.concatenate(left, axis=1)
                term = jnp.dot(left, weight[...], preferred_element_type=F32)
                total = term if total is None else total + term
            outs[2 * side + part][...] = total


def multiply(hidden, hidden_other, pieces, core, totals):
    sources = []
    uses = []
    for blocks, part, _ in pieces:
        cols = []
        for block in blocks:
            known = [k for k, (name, _) in enumerate(sources) if name == block[0]]
            if known:
                cols.append(known[0])
            else:
                cols.append(len(sources))
                sources.append(block)
        uses.append((tuple(cols), part))
    n_h = len(sources)
    index = jnp.stack([s[1] for s in sources] + [core]).astype(jnp.int32)
    own_specs = [
        pl.BlockSpec(
            (TOK, ROWS), functools.partial(lambda k, i, at: (0, 2 * at[k] + at[n_h]), k)
        )
        for k in range(n_h)
    ]
    other_specs = [
        pl.BlockSpec((TOK, ROWS), functools.partial(lambda k, i, at: (0, at[k]), k))
        for k in range(n_h)
    ]
    weights = [p[2] for p in pieces]
    whole = pl.BlockSpec(memory_space=pltpu.VMEM)
    n_t = 0 if totals is None else 4
    depth = sum(w.shape[0] for w in weights)
    return pl.pallas_call(
        functools.partial(multiply_kernel, n_h, uses),
        out_shape=[jax.ShapeDtypeStruct((TOK, HALF), F32)] * 4,
        grid_spec=pltpu.PrefetchScalarGridSpec(
            num_scalar_prefetch=1,
            grid=(1,),
            in_specs=own_specs + other_specs + [whole] * (len(weights) + n_t),
            out_specs=[whole] * 4,
        ),
        input_output_aliases={1 + 2 * n_h + len(weights) + k: k for k in range(n_t)},
        cost_estimate=pl.CostEstimate(
            flops=4 * TOK * depth * HALF,
            bytes_accessed=2 * depth * HALF + 4 * TOK * depth,
            transcendentals=0,
        ),
        compiler_params=pltpu.CompilerParams(vmem_limit_bytes=20 * 2**20),
    )(
        index,
        *([hidden] * n_h),
        *([hidden_other] * n_h),
        *weights,
        *(totals or ()),
    )


def rope(head, cosine, sine):
    return head * cosine + pltpu.roll(head, HEAD // 2, 1) * sine


def rotate_kernel(query_ref, cos_ref, sin_ref, out_ref):
    for h in range(GROUP_HEADS):
        cols = slice(h * HEAD, (h + 1) * HEAD)
        out_ref[:, cols] = rope(
            query_ref[:, cols].astype(F32), cos_ref[...], sin_ref[...]
        ).astype(BF16)


def rotate_queries(queries, cosine, sine):
    width = GROUP_HEADS * HEAD
    spec = pl.BlockSpec((TOK, width), lambda h: (0, h))
    table = pl.BlockSpec((TOK, HEAD), lambda h: (0, 0))
    return pl.pallas_call(
        rotate_kernel,
        out_shape=jax.ShapeDtypeStruct(queries.shape, BF16),
        grid=(KV_HEADS,),
        in_specs=[spec, table, table],
        out_specs=spec,
        cost_estimate=pl.CostEstimate(
            flops=4 * queries.size, bytes_accessed=4 * queries.size, transcendentals=0
        ),
    )(queries, cosine, sine)


def attend_kernel(
    query_ref, key_ref, key_add_ref, val_ref, val_add_ref, cos_ref, sin_ref, bias_ref, out_ref
):
    keys = rope(key_ref[...] + key_add_ref[...], cos_ref[...], sin_ref[...]).astype(BF16)
    vals = (val_ref[...] + val_add_ref[...]).astype(BF16)
    vals = jnp.concatenate([vals, jnp.ones((TOK, HEAD), BF16)], axis=1)
    factor = math.log2(math.e) / math.sqrt(HEAD)
    part = TOK // 2
    for h in range(GROUP_HEADS):
        cols = slice(h * HEAD, (h + 1) * HEAD)
        for r in range(2):
            rows = slice(r * part, (r + 1) * part)
            seen = (r + 1) * part
            scores = lax.dot_general(
                query_ref[rows, cols],
                keys[:seen],
                (((1,), (1,)), ((), ())),
                preferred_element_type=F32,
            )
            scores = scores + bias_ref[rows, :seen]
            peak = jnp.max(scores, axis=1, keepdims=True)
            weights = jnp.exp2((scores - peak) * factor).astype(BF16)
            both = jnp.dot(weights, vals[:seen], preferred_element_type=F32)
            out_ref[rows, cols] = (both[:, :HEAD] / both[:, HEAD:]).astype(BF16)


def attend(rotated, keys, keys_add, vals, vals_add, cosine, sine, bias):
    width = GROUP_HEADS * HEAD
    wide = pl.BlockSpec((TOK, width), lambda h: (0, h))
    one = pl.BlockSpec((TOK, HEAD), lambda h: (0, h))
    table = pl.BlockSpec((TOK, HEAD), lambda h: (0, 0))
    square = pl.BlockSpec((TOK, TOK), lambda h: (0, 0))
    return pl.pallas_call(
        attend_kernel,
        out_shape=jax.ShapeDtypeStruct(rotated.shape, BF16),
        grid=(KV_HEADS,),
        in_specs=[wide, one, one, one, one, table, table, square],
        out_specs=wide,
        cost_estimate=pl.CostEstimate(
            flops=4 * rotated.size * TOK,
            bytes_accessed=4 * rotated.size,
            transcendentals=rotated.size * 2,
        ),
        compiler_params=pltpu.CompilerParams(vmem_limit_bytes=24 * 2**20),
    )(rotated, keys, keys_add, vals, vals_add, cosine, sine, bias)


def tables(token_row):
    token = jnp.arange(TOK, dtype=jnp.int32)
    started = (token_row == BOS)[None, :] & (token[None, :] <= token[:, None])
    latest = jnp.max(jnp.where(started, token[None, :], 0), axis=1)
    positions = (token - latest).astype(F32)
    steps = jnp.arange(HEAD // 2, dtype=F32)
    inverse = rope_base ** (-2.0 * steps / HEAD)
    angles = positions[:, None] * inverse[None, :]
    cosine, sine = jnp.cos(angles), jnp.sin(angles)
    allowed = (token[None, :] <= token[:, None]) & (token[None, :] >= latest[:, None])
    bias = jnp.where(allowed, 0.0, -1e30).astype(F32)
    return (
        jnp.concatenate([cosine, cosine], axis=1),
        jnp.concatenate([-sine, sine], axis=1),
        bias,
    )


def top_bit(number):
    return 31 - lax.clz(jnp.maximum(number, 1))


def power(exponent):
    return lax.shift_left(jnp.full(exponent.shape, 1, jnp.int32), exponent).astype(F32)


def encode_kernel(base_ref, weight_ref, out_ref):
    lanes = lax.broadcasted_iota(jnp.int32, (base_ref.shape[0], HEAD), 1)
    for j in range(base_ref.shape[1] // HEAD):
        cols = slice(j * HEAD, (j + 1) * HEAD)
        delta = base_ref[:, cols] - weight_ref[:, cols].astype(F32)
        size = jnp.abs(delta)
        peak = size
        for reach in (1, 2, 4, 8, 16):
            beside = jnp.where(
                (lanes & reach) != 0,
                pltpu.roll(peak, reach, 1),
                pltpu.roll(peak, HEAD - reach, 1),
            )
            peak = jnp.maximum(peak, beside)
        block = top_bit((peak * 2.0**30).astype(jnp.int32))
        scale = power(block) * 2.0**-38
        value = size * (power(30 - block) * 2.0**8)
        step = top_bit((value * 2.0**6).astype(jnp.int32))
        counted = jnp.floor(value * (power(14 - step) * 2.0**-5) + 0.5)
        code = jnp.minimum(counted * (power(step) * 2.0**-9), 448.0) * scale
        out_ref[:, cols] = jnp.where(delta < 0, -code, code).astype(BF16)


def encode(base, weights):
    rows, width = base.shape
    tall = rows // 2
    spec = pl.BlockSpec((tall, width), lambda i: (i, 0))
    return pl.pallas_call(
        encode_kernel,
        out_shape=jax.ShapeDtypeStruct(base.shape, BF16),
        grid=(2,),
        in_specs=[spec, spec],
        out_specs=spec,
        cost_estimate=pl.CostEstimate(
            flops=40 * base.size, bytes_accessed=8 * base.size, transcendentals=0
        ),
    )(base, weights)


def body(
    hidden_states, queries, token_ids, local_weights, outer_base, momentum, outer_rates, frag_index
):
    own = local_weights[0]
    place = lax.axis_index("fsdp")
    z, y, core = place // (Y_HI * CORES), (place // CORES) % Y_HI, place % CORES

    def near(dz, dy):
        return ((dz % Z, dy), ((z + dz) % Z) * Y_HI + (y + dy) % Y_HI)

    keys, vals = own[:, :HALF], own[:, HALF:]
    keys_across = send(keys, ACROSS)
    vals_up, vals_down = [send(vals, UP)], [send(vals, DOWN)]
    hidden_other = send(pick_columns(hidden_states, core[None]), SWAP)
    decoded = encode(outer_base, own)
    summed = lax.all_gather(
        decoded, "rep", axis_index_groups=[list(range(X)), list(range(X, 2 * X))]
    )
    cosine, sine, bias = tables(token_ids)

    pair = jnp.concatenate([keys, keys_across], axis=0)
    pair_up, pair_down = [send(pair, UP)], [send(pair, DOWN)]
    vals_, pair = tie(vals, pair)
    across = [send(vals_, ACROSS)]
    rotated = rotate_queries(queries, cosine, sine)
    vals_up.append(send(vals_up[0], UP))
    vals_down.append(send(vals_down[0], DOWN))
    both, across[0] = tie(jnp.concatenate([vals_up[0], vals_down[0]], axis=0), across[0])
    across.append(send(both, ACROSS))
    pair_up.append(send(pair_up[0], UP))
    pair_down.append(send(pair_down[0], DOWN))
    vals_up.append(send(vals_up[1], UP))
    vals_down.append(send(vals_down[1], DOWN))
    both, across[1] = tie(jnp.concatenate([vals_up[1], vals_down[1]], axis=0), across[1])
    across.append(send(both, ACROSS))
    pair_up.append(send(pair_up[1], UP))
    pair_down.append(send(pair_down[1], DOWN))
    vals_down.append(send(vals_down[2], DOWN))
    both, across[2] = tie(jnp.concatenate([vals_up[2], vals_down[2]], axis=0), across[2])
    across.append(send(both, ACROSS))
    pair_up.append(send(pair_up[2], UP))
    last, across[3] = tie(vals_down[3], across[3])
    across.append(send(last, ACROSS))

    def two(dz):
        return [near(dz, 0), near(dz, 1)]

    totals = multiply(
        hidden_states,
        hidden_other,
        [
            (two(0), 0, pair),
            (two(-1), 0, pair_up[0]),
            (two(1), 0, pair_down[0]),
            ([near(0, 0)], 1, vals),
            ([near(0, 1)], 1, across[0]),
            ([near(-1, 0)], 1, vals_up[0]),
            ([near(1, 0)], 1, vals_down[0]),
        ],
        core,
        None,
    )
    totals = multiply(
        hidden_states,
        hidden_other,
        [
            (two(-2), 0, pair_up[1]),
            (two(2), 0, pair_down[1]),
            ([near(-1, 1), near(1, 1)], 1, across[1]),
            ([near(-2, 0)], 1, vals_up[1]),
            ([near(2, 0)], 1, vals_down[1]),
        ],
        core,
        totals,
    )
    totals = multiply(
        hidden_states,
        hidden_other,
        [
            (two(-3), 0, pair_up[2]),
            (two(3), 0, pair_down[2]),
            ([near(-2, 1), near(2, 1)], 1, across[2]),
            ([near(-3, 0)], 1, vals_up[2]),
            ([near(3, 0)], 1, vals_down[2]),
        ],
        core,
        totals,
    )
    totals = multiply(
        hidden_states,
        hidden_other,
        [
            (two(-4), 0, pair_up[3]),
            ([near(-3, 1), near(3, 1)], 1, across[3]),
            ([near(4, 0)], 1, vals_down[3]),
            ([near(4, 1)], 1, across[4]),
        ],
        core,
        totals,
    )
    key_own, val_own, key_other, val_other = totals
    key_add, val_add = send(key_other, SWAP), send(val_other, SWAP)
    context = attend(rotated, key_own, key_add, val_own, val_add, cosine, sine, bias)

    groups = lax.axis_size("rep")
    part = jnp.sum(summed.astype(F32), axis=0).astype(BF16)
    rest = lax.ppermute(part, "rep", [(i, (i + X) % groups) for i in range(groups)])
    outer_grad = (part.astype(F32) + rest.astype(F32)) / groups
    table = jnp.arange(outer_rates.shape[0], dtype=jnp.int32)
    rate = jnp.sum(jnp.where(table == frag_index[0], outer_rates, 0.0))
    new_momentum = momentum_coef * momentum + outer_grad
    new_base = outer_base - rate * (outer_grad + momentum_coef * new_momentum)
    return (context, new_base, new_momentum)


def solution(mesh):
    placed = (
        P(("rep", "fsdp"), None),
        P(("rep", "fsdp"), None),
        P(("rep", "fsdp")),
        P("rep", "fsdp", None),
        P("fsdp", None),
        P("fsdp", None),
        P(),
        P(),
    )
    return jax.shard_map(
        body,
        mesh=mesh,
        in_specs=placed,
        out_specs=(P(("rep", "fsdp"), None), P("fsdp", None), P("fsdp", None)),
        check_vma=False,
    )
```

```python
import functools
import math

import jax
import jax.numpy as jnp
from jax import lax
from jax.experimental import pallas as pl
from jax.experimental.pallas import tpu as pltpu
from jax.sharding import PartitionSpec as P

HEAD = 128
BLOCK = 32
BOS = 128000
TOK = 256
ROWS = 256
KV_HEADS = 4
HALF = KV_HEADS * HEAD
GROUP_HEADS = 8
Z, Y_HI, CORES = 8, 2, 2
X = 4

rope_base = 500000.0
momentum_coef = 0.9
F32 = jnp.float32
BF16 = jnp.bfloat16

NO_COST = pl.CostEstimate(flops=0, bytes_accessed=0, transcendentals=0)


def fsdp_pairs(move):
    pairs = []
    for z in range(Z):
        for y in range(Y_HI):
            for c in range(CORES):
                z2, y2, c2 = move(z, y, c)
                pairs.append(
                    (
                        (z * Y_HI + y) * CORES + c,
                        ((z2 % Z) * Y_HI + y2 % Y_HI) * CORES + c2 % CORES,
                    )
                )
    return pairs


UP = fsdp_pairs(lambda z, y, c: (z + 1, y, c))
DOWN = fsdp_pairs(lambda z, y, c: (z - 1, y, c))
ACROSS = fsdp_pairs(lambda z, y, c: (z, y + 1, c))
SWAP = fsdp_pairs(lambda z, y, c: (z, y, c + 1))


def send(block, pairs):
    return lax.ppermute(block, "fsdp", pairs)


def tie(*arrays):
    return lax.optimization_barrier(arrays)


def collect_kernel(moves, n_in, *refs):
    sources, (*outs, sems) = refs[:n_in], refs[n_in:]
    copies = []
    for i, (source, col, out, at) in enumerate(moves):
        copies.append(
            pltpu.make_async_copy(
                sources[source].at[:, pl.ds(col, HALF)],
                outs[out].at[pl.ds(at, ROWS), :],
                sems.at[i],
            )
        )
        copies[-1].start()
    for copy in copies:
        copy.wait()


def collect(sources, outs):
    moves = []
    for out, pieces in enumerate(outs):
        for i, (source, col) in enumerate(pieces):
            moves.append((source, col, out, i * ROWS))
    return pl.pallas_call(
        functools.partial(collect_kernel, moves, len(sources)),
        out_shape=[jax.ShapeDtypeStruct((len(p) * ROWS, HALF), BF16) for p in outs],
        in_specs=[pl.BlockSpec(memory_space=pltpu.HBM)] * len(sources),
        out_specs=[pl.BlockSpec(memory_space=pltpu.VMEM)] * len(outs),
        scratch_shapes=[pltpu.SemaphoreType.DMA((len(moves),))],
        cost_estimate=NO_COST,
        compiler_params=pltpu.CompilerParams(vmem_limit_bytes=2 * 2**20),
    )(*sources)


def block_place(place_ref, dz, dy):
    z, y, core = place_ref[0], place_ref[1], place_ref[2]
    return (lax.rem(z + dz + Z, Z) * Y_HI + lax.rem(y + dy, Y_HI)) * CORES + core


def multiply_kernel(blocks, moves, spans, n_w, add, ahead, place_ref, *refs):
    hidden = refs[:2]
    weights = refs[2 : 2 + n_w]
    before = refs[2 + n_w : 2 + n_w + add]
    out_ref = refs[2 + n_w + add]
    if ahead:
        ahead_ref = refs[3 + n_w + add]
        refs = refs[4 + n_w + add :]
    else:
        refs = refs[3 + n_w + add :]
    states, stacks, (held, out_sems, sems) = refs[0], refs[1:3], refs[3:]
    count = iter(range(sems.shape[0]))

    def begin(source, target):
        copy = pltpu.make_async_copy(source, target, sems.at[next(count)])
        copy.start()
        return copy

    def fetch(block, target, slot):
        start = pl.multiple_of(block_place(place_ref, *block) * ROWS, ROWS)
        return [
            begin(
                hidden[side].at[:, pl.ds(start, ROWS)],
                target.at[pl.ds(side * TOK, TOK), pl.ds(slot * ROWS, ROWS)],
            )
            for side in range(2)
        ]

    ready = []
    for slot, block in enumerate(blocks):
        ready += fetch(block, states, slot)
    parts = []
    for part in range(2):
        copies = []
        for piece, row, col, slot in moves[part]:
            copies.append(
                begin(
                    weights[piece].at[pl.ds(row, ROWS), pl.ds(col, HALF)],
                    stacks[part].at[pl.ds(slot, ROWS), :],
                )
            )
        if add:
            copies.append(begin(before[0].at[part], held.at[part]))
        parts.append(copies)
    later = []
    for slot, block in enumerate(ahead):
        later += fetch(block, ahead_ref, slot)
    for copy in ready:
        copy.wait()
    leaving = []
    for part in range(2):
        for copy in parts[part]:
            copy.wait()
        first, last = spans[part]
        for half in range(2):
            cols = slice(half * ROWS, (half + 1) * ROWS)
            total = jnp.dot(
                states[:, first * ROWS : last * ROWS],
                stacks[part][:, cols],
                preferred_element_type=F32,
            )
            if add:
                total = total + held[part, :, cols]
            if ahead:
                out_ref[part, :, cols] = total
            else:
                held[part, :, cols] = total
        if not ahead:
            copy = pltpu.make_async_copy(held.at[part], out_ref.at[part], out_sems.at[part])
            copy.start()
            leaving.append(copy)
    for copy in later + leaving:
        copy.wait()


def multiply(hidden, hidden_other, blocks, pieces, place, total=None, ahead=()):
    weights, moves, spans = [], [], []
    for which, part in enumerate(pieces):
        slots = [slot for _, places in part for slot in places]
        first, last = min(slots), max(slots) + 1
        assert sorted(slots) == list(range(first, last))
        spans.append((first, last))
        moves.append([])
        for rows, places in part:
            col = which * HALF if rows.shape[1] > HALF else 0
            for i, slot in enumerate(places):
                moves[-1].append((len(weights), i * ROWS, col, (slot - first) * ROWS))
            weights.append(rows)
    n_h, n_w, n_a = len(blocks), len(weights), len(ahead)
    add = 0 if total is None else 1
    far = pl.BlockSpec(memory_space=pltpu.HBM)
    near = pl.BlockSpec(memory_space=pltpu.VMEM)
    n_sems = 2 * (n_h + n_a) + sum(len(m) for m in moves) + 2 * add
    scratch = [pltpu.VMEM((2 * TOK, n_h * ROWS), BF16)]
    scratch += [pltpu.VMEM(((last - first) * ROWS, HALF), BF16) for first, last in spans]
    scratch += [
        pltpu.VMEM((2, 2 * TOK, HALF), F32),
        pltpu.SemaphoreType.DMA((2,)),
        pltpu.SemaphoreType.DMA((n_sems,)),
    ]
    out_shape = [jax.ShapeDtypeStruct((2, 2 * TOK, HALF), F32)]
    if ahead:
        out_shape.append(jax.ShapeDtypeStruct((2 * TOK, n_a * ROWS), BF16))
    return pl.pallas_call(
        functools.partial(multiply_kernel, blocks, moves, spans, n_w, add, ahead),
        out_shape=out_shape,
        in_specs=[pl.BlockSpec(memory_space=pltpu.SMEM)] + [far] * (2 + n_w + add),
        out_specs=[near] * 2 if ahead else [far],
        scratch_shapes=scratch,
        cost_estimate=NO_COST,
        compiler_params=pltpu.CompilerParams(vmem_limit_bytes=(48 if ahead else 60) * 2**20),
    )(place, hidden, hidden_other, *weights, *([total] * add))


def finish_kernel(
    states_ref, total_ref, near_ref, far_ref, val_in_ref,
    key_ref, val_ref, key_swap_ref, val_swap_ref
):
    uses = ((near_ref, 0, 0), (far_ref, 0, 1), (val_in_ref, 1, 0))
    outs = ((key_ref, key_swap_ref), (val_ref, val_swap_ref))
    for part in range(2):
        for half in range(2):
            cols = slice(half * ROWS, (half + 1) * ROWS)
            total = total_ref[part, :, cols]
            for ref, where, slot in uses:
                if where == part:
                    total = total + jnp.dot(
                        states_ref[:, slot * ROWS : (slot + 1) * ROWS],
                        ref[:, cols],
                        preferred_element_type=F32,
                    )
            mine_ref, swap_ref = outs[part]
            mine_ref[:, cols] = total[:TOK]
            swap_ref[:, cols] = total[TOK:].astype(swap_ref.dtype)


def finish(states, total, keys_near, keys_far, vals):
    near = pl.BlockSpec(memory_space=pltpu.VMEM)
    return pl.pallas_call(
        finish_kernel,
        out_shape=[
            jax.ShapeDtypeStruct((TOK, HALF), F32),
            jax.ShapeDtypeStruct((TOK, HALF), F32),
            jax.ShapeDtypeStruct((TOK, HALF), F32),
            jax.ShapeDtypeStruct((TOK, HALF), BF16),
        ],
        in_specs=[near] * 5,
        out_specs=[near] * 4,
        cost_estimate=NO_COST,
        compiler_params=pltpu.CompilerParams(vmem_limit_bytes=6 * 2**20),
    )(states, total, keys_near, keys_far, vals)


def rope(head, cosine, sine):
    return head * cosine + pltpu.roll(head, HEAD // 2, 1) * sine


def rotate_kernel(query_ref, cos_ref, sin_ref, out_ref):
    for h in range(GROUP_HEADS):
        cols = slice(h * HEAD, (h + 1) * HEAD)
        out_ref[:, cols] = rope(
            query_ref[:, cols].astype(F32), cos_ref[...], sin_ref[...]
        ).astype(BF16)


def rotate_queries(queries, cosine, sine):
    width = GROUP_HEADS * HEAD
    spec = pl.BlockSpec((TOK, width), lambda h: (0, h))
    table = pl.BlockSpec((TOK, HEAD), lambda h: (0, 0))
    return pl.pallas_call(
        rotate_kernel,
        out_shape=jax.ShapeDtypeStruct(queries.shape, BF16),
        grid=(KV_HEADS,),
        in_specs=[spec, table, table],
        out_specs=spec,
        cost_estimate=NO_COST,
        compiler_params=pltpu.CompilerParams(vmem_limit_bytes=6 * 2**20),
    )(queries, cosine, sine)


def attend_kernel(
    query_ref, key_ref, key_add_ref, val_ref, val_add_ref, cos_ref, sin_ref, bias_ref, out_ref
):
    keys = rope(key_ref[...] + key_add_ref[...], cos_ref[...], sin_ref[...]).astype(BF16)
    vals = (val_ref[...] + val_add_ref[...].astype(F32)).astype(BF16)
    vals = jnp.concatenate([vals, jnp.ones((TOK, HEAD), BF16)], axis=1)
    factor = math.log2(math.e) / math.sqrt(HEAD)
    part = TOK // 2
    for r in range(2):
        rows = slice(r * part, (r + 1) * part)
        seen = (r + 1) * part
        heads = [query_ref[rows, h * HEAD : (h + 1) * HEAD] for h in range(GROUP_HEADS)]
        scores = lax.dot_general(
            jnp.concatenate(heads, axis=0),
            keys[:seen],
            (((1,), (1,)), ((), ())),
            preferred_element_type=F32,
        )
        scores = scores.reshape(GROUP_HEADS, part, seen) + bias_ref[rows, :seen][None]
        peak = jnp.max(scores, axis=2, keepdims=True)
        weights = jnp.exp2((scores - peak) * factor).astype(BF16)
        both = jnp.dot(
            weights.reshape(GROUP_HEADS * part, seen),
            vals[:seen],
            preferred_element_type=F32,
        )
        context = (both[:, :HEAD] / both[:, HEAD:]).astype(BF16)
        for h in range(GROUP_HEADS):
            out_ref[rows, h * HEAD : (h + 1) * HEAD] = context[h * part : (h + 1) * part]


def attend(rotated, keys, keys_add, vals, vals_add, cosine, sine, bias):
    width = GROUP_HEADS * HEAD
    wide = pl.BlockSpec((TOK, width), lambda h: (0, h))
    one = pl.BlockSpec((TOK, HEAD), lambda h: (0, h))
    table = pl.BlockSpec((TOK, HEAD), lambda h: (0, 0))
    square = pl.BlockSpec((TOK, TOK), lambda h: (0, 0))
    return pl.pallas_call(
        attend_kernel,
        out_shape=jax.ShapeDtypeStruct(rotated.shape, BF16),
        grid=(KV_HEADS,),
        in_specs=[wide, one, one, one, one, table, table, square],
        out_specs=wide,
        cost_estimate=NO_COST,
        compiler_params=pltpu.CompilerParams(vmem_limit_bytes=12 * 2**20),
    )(rotated, keys, keys_add, vals, vals_add, cosine, sine, bias)


def tables(token_row):
    token = jnp.arange(TOK, dtype=jnp.int32)
    started = (token_row == BOS)[None, :] & (token[None, :] <= token[:, None])
    latest = jnp.max(jnp.where(started, token[None, :], 0), axis=1)
    positions = (token - latest).astype(F32)
    steps = jnp.arange(HEAD // 2, dtype=F32)
    inverse = rope_base ** (-2.0 * steps / HEAD)
    angles = positions[:, None] * inverse[None, :]
    cosine, sine = jnp.cos(angles), jnp.sin(angles)
    allowed = (token[None, :] <= token[:, None]) & (token[None, :] >= latest[:, None])
    bias = jnp.where(allowed, 0.0, -1e30).astype(F32)
    return (
        jnp.concatenate([cosine, cosine], axis=1),
        jnp.concatenate([-sine, sine], axis=1),
        bias,
    )


def top_bit(number):
    return 31 - lax.clz(jnp.maximum(number, 1))


def power(exponent):
    return lax.shift_left(jnp.full(exponent.shape, 1, jnp.int32), exponent).astype(F32)


def encode_kernel(base_ref, weight_ref, out_ref):
    lanes = lax.broadcasted_iota(jnp.int32, (base_ref.shape[0], HEAD), 1)
    for j in range(base_ref.shape[1] // HEAD):
        cols = slice(j * HEAD, (j + 1) * HEAD)
        delta = base_ref[:, cols] - weight_ref[:, cols].astype(F32)
        size = jnp.abs(delta)
        peak = size
        for reach in (1, 2, 4, 8, 16):
            peak = jnp.maximum(peak, pltpu.roll(peak, reach, 1))
        peak = jnp.take_along_axis(peak, lanes | (BLOCK - 1), axis=1)
        block = top_bit((peak * 2.0**30).astype(jnp.int32))
        value = (size * (power(30 - block) * 2.0**29)).astype(jnp.int32)
        step = jnp.maximum(top_bit(value), 15) - 3
        half = lax.shift_left(jnp.full(step.shape, 1, jnp.int32), step - 1)
        counted = lax.shift_right_logical(value + half, step)
        value = jnp.minimum(lax.shift_left(counted, step), 448 * 2**21)
        code = value.astype(F32) * (power(block) * 2.0**-59)
        out_ref[:, cols] = jnp.where(delta < 0, -code, code).astype(BF16)


def encode(base, weights):
    rows, width = base.shape
    tall = rows // 2
    spec = pl.BlockSpec((tall, width), lambda i: (i, 0))
    return pl.pallas_call(
        encode_kernel,
        out_shape=jax.ShapeDtypeStruct(base.shape, BF16),
        grid=(2,),
        in_specs=[spec, spec],
        out_specs=spec,
        cost_estimate=NO_COST,
        compiler_params=pltpu.CompilerParams(vmem_limit_bytes=6 * 2**20),
    )(base, weights)


def body(
    hidden_states, queries, token_ids, local_weights, outer_base, momentum, outer_rates, frag_index
):
    own = local_weights[0]
    place = lax.axis_index("fsdp")
    z, y, core = place // (Y_HI * CORES), (place // CORES) % Y_HI, place % CORES

    place = jnp.stack([z, y, core]).astype(jnp.int32)

    groups = lax.axis_size("rep")

    def along_x(pick):
        return [(i, i // X * X + pick(i % X)) for i in range(groups)]

    def add(mine, theirs):
        return (mine.astype(F32) + theirs.astype(F32)).astype(BF16)

    hidden_other = send(hidden_states, SWAP)
    up, down = [send(own, UP)], [send(own, DOWN)]
    keys_across = send(own[:, :HALF], ACROSS)
    across = [send(own[:, HALF:], ACROSS)]

    def halves(*blocks):
        return collect(blocks, [[(i, HALF) for i in range(len(blocks))]])[0]

    hidden_other, own_ = tie(hidden_other, own)
    decoded = encode(outer_base, own_)
    up[0], down[0], keys_across, decoded, queries, token_ids = tie(
        up[0], down[0], keys_across, decoded, queries, token_ids
    )
    up.append(send(up[0], UP))
    down.append(send(down[0], DOWN))
    far_up = [send(keys_across, UP)]
    rest = lax.ppermute(decoded, "rep", along_x(lambda x: x ^ 1))
    across.append(send(halves(up[0], down[0]), ACROSS))

    cosine, sine, bias = tables(token_ids)
    table = jnp.arange(outer_rates.shape[0], dtype=jnp.int32)
    rate = jnp.sum(jnp.where(table == frag_index[0], outer_rates, 0.0))
    rotated = rotate_queries(queries, cosine, sine)

    (total,) = multiply(
        hidden_states,
        hidden_other,
        [(0, 0), (0, 1), (-1, 0), (1, 0)],
        [
            [(own, (0,)), (keys_across, (1,)), (up[0], (2,)), (down[0], (3,))],
            [(own, (0,)), (across[0], (1,)), (up[0], (2,)), (down[0], (3,))],
        ],
        place,
    )
    up[1], down[1], rotated, total, rate = tie(up[1], down[1], rotated, total, rate)
    up.append(send(up[1], UP))
    down.append(send(down[1], DOWN))
    up[1], down[1], far_up[0], across[1], rest, keys_across = tie(
        up[1], down[1], far_up[0], across[1], rest, keys_across
    )
    far_up.append(send(far_up[0], UP))
    far_down = [send(keys_across, DOWN)]
    across.append(send(halves(up[1], down[1]), ACROSS))
    part = add(decoded, rest)
    (total,) = multiply(
        hidden_states,
        hidden_other,
        [(-1, 1), (-2, 0), (2, 0), (1, 1)],
        [
            [(far_up[0], (0,)), (up[1], (1,)), (down[1], (2,))],
            [(across[1], (0, 3)), (up[1], (1,)), (down[1], (2,))],
        ],
        place,
        total,
    )
    up[2], down[2], total, part = tie(up[2], down[2], total, part)
    val_last, key_last, vals = collect(
        (up[2], down[2]), [[(0, HALF)], [(1, 0)], [(0, HALF), (1, HALF)]]
    )
    val_last = send(val_last, UP)
    key_last = send(key_last, DOWN)
    up[2], down[2], far_up[1], far_down[0], across[2], vals = tie(
        up[2], down[2], far_up[1], far_down[0], across[2], vals
    )
    far_up.append(send(far_up[1], UP))
    far_down.append(send(far_down[0], DOWN))
    across.append(send(vals, ACROSS))

    (total,) = multiply(
        hidden_states,
        hidden_other,
        [(1, 1), (-2, 1), (-3, 0), (3, 0), (2, 1)],
        [
            [(far_down[0], (0,)), (far_up[1], (1,)), (up[2], (2,)), (down[2], (3,))],
            [(across[2], (1, 4)), (up[2], (2,)), (down[2], (3,))],
        ],
        place,
        total,
    )
    val_last, key_last, total = tie(val_last, key_last, total)
    across.append(send(val_last, ACROSS))
    val_last, key_last, far_up[2], far_down[1], across[3], part = tie(
        val_last, key_last, far_up[2], far_down[1], across[3], part
    )
    far_up.append(send(far_up[2], UP))
    far_down.append(send(far_down[1], DOWN))
    rest = lax.ppermute(part, "rep", along_x(lambda x: X - 1 - x))
    total, states = multiply(
        hidden_states,
        hidden_other,
        [(2, 1), (-3, 1), (4, 0), (3, 1)],
        [
            [(far_down[1], (0,)), (far_up[2], (1,)), (key_last, (2,))],
            [(across[3], (1, 3)), (val_last, (2,))],
        ],
        place,
        total,
        ahead=((4, 1), (3, 1)),
    )
    key_own, val_own, key_swap, val_swap = finish(
        states, total, far_up[3], far_down[2], across[4]
    )
    rest, key_own = tie(rest, key_own)
    part = add(part, rest)
    rest = lax.ppermute(part, "rep", [(i, (i + X) % groups) for i in range(groups)])
    key_add, val_add = send(key_swap, SWAP), send(val_swap, SWAP)
    context = attend(rotated, key_own, key_add, val_own, val_add, cosine, sine, bias)
    context, rest = tie(context, rest)
    outer_grad = (part.astype(F32) + rest.astype(F32)) / groups
    new_momentum = momentum_coef * momentum + outer_grad
    new_base = outer_base - rate * (outer_grad + momentum_coef * new_momentum)
    return (context, new_base, new_momentum)


def solution(mesh):
    placed = (
        P(("rep", "fsdp"), None),
        P(("rep", "fsdp"), None),
        P(("rep", "fsdp")),
        P("rep", "fsdp", None),
        P("fsdp", None),
        P("fsdp", None),
        P(),
        P(),
    )
    return jax.shard_map(
        body,
        mesh=mesh,
        in_specs=placed,
        out_specs=(P(("rep", "fsdp"), None), P("fsdp", None), P("fsdp", None)),
        check_vma=False,
    )
```

```python
import functools
import math

import jax
import jax.numpy as jnp
from jax import lax
from jax.experimental import pallas as pl
from jax.experimental.pallas import tpu as pltpu
from jax.sharding import PartitionSpec as P

HEAD = 128
BLOCK = 32
BOS = 128000
TOK = 256
ROWS = 256
KV_HEADS = 4
HALF = KV_HEADS * HEAD
GROUP_HEADS = 8
Z, Y_HI, CORES = 8, 2, 2
X = 4

rope_base = 500000.0
momentum_coef = 0.9
F32 = jnp.float32
BF16 = jnp.bfloat16

NO_COST = pl.CostEstimate(flops=0, bytes_accessed=0, transcendentals=0)


def fsdp_pairs(move):
    pairs = []
    for z in range(Z):
        for y in range(Y_HI):
            for c in range(CORES):
                z2, y2, c2 = move(z, y, c)
                pairs.append(
                    (
                        (z * Y_HI + y) * CORES + c,
                        ((z2 % Z) * Y_HI + y2 % Y_HI) * CORES + c2 % CORES,
                    )
                )
    return pairs


UP = fsdp_pairs(lambda z, y, c: (z + 1, y, c))
DOWN = fsdp_pairs(lambda z, y, c: (z - 1, y, c))
ACROSS = fsdp_pairs(lambda z, y, c: (z, y + 1, c))
SWAP = fsdp_pairs(lambda z, y, c: (z, y, c + 1))


def send(block, pairs):
    return lax.ppermute(block, "fsdp", pairs)


def tie(*arrays):
    return lax.optimization_barrier(arrays)


def collect_kernel(moves, n_in, *refs):
    sources, (*outs, sems) = refs[:n_in], refs[n_in:]
    copies = []
    for i, (source, col, out, at) in enumerate(moves):
        copies.append(
            pltpu.make_async_copy(
                sources[source].at[:, pl.ds(col, HALF)],
                outs[out].at[pl.ds(at, ROWS), :],
                sems.at[i],
            )
        )
        copies[-1].start()
    for copy in copies:
        copy.wait()


def collect(sources, outs):
    moves = []
    for out, pieces in enumerate(outs):
        for i, (source, col) in enumerate(pieces):
            moves.append((source, col, out, i * ROWS))
    return pl.pallas_call(
        functools.partial(collect_kernel, moves, len(sources)),
        out_shape=[jax.ShapeDtypeStruct((len(p) * ROWS, HALF), BF16) for p in outs],
        in_specs=[pl.BlockSpec(memory_space=pltpu.HBM)] * len(sources),
        out_specs=[pl.BlockSpec(memory_space=pltpu.VMEM)] * len(outs),
        scratch_shapes=[pltpu.SemaphoreType.DMA((len(moves),))],
        cost_estimate=NO_COST,
        compiler_params=pltpu.CompilerParams(vmem_limit_bytes=2 * 2**20),
    )(*sources)


def block_place(place_ref, dz, dy):
    z, y, core = place_ref[0], place_ref[1], place_ref[2]
    return (lax.rem(z + dz + Z, Z) * Y_HI + lax.rem(y + dy, Y_HI)) * CORES + core


def multiply_kernel(blocks, moves, spans, n_w, add, ahead, place_ref, *refs):
    hidden = refs[:2]
    weights = refs[2 : 2 + n_w]
    before = refs[2 + n_w : 2 + n_w + add]
    out_ref = refs[2 + n_w + add]
    if ahead:
        ahead_ref = refs[3 + n_w + add]
        refs = refs[4 + n_w + add :]
    else:
        refs = refs[3 + n_w + add :]
    states, stacks, (held, out_sems, sems) = refs[0], refs[1:3], refs[3:]
    count = iter(range(sems.shape[0]))

    def begin(source, target):
        copy = pltpu.make_async_copy(source, target, sems.at[next(count)])
        copy.start()
        return copy

    def fetch(block, target, slot):
        start = pl.multiple_of(block_place(place_ref, *block) * ROWS, ROWS)
        return [
            begin(
                hidden[side].at[:, pl.ds(start, ROWS)],
                target.at[pl.ds(side * TOK, TOK), pl.ds(slot * ROWS, ROWS)],
            )
            for side in range(2)
        ]

    ready = []
    for slot, block in enumerate(blocks):
        ready += fetch(block, states, slot)
    parts = []
    for part in range(2):
        copies = []
        for piece, row, col, slot in moves[part]:
            copies.append(
                begin(
                    weights[piece].at[pl.ds(row, ROWS), pl.ds(col, HALF)],
                    stacks[part].at[pl.ds(slot, ROWS), :],
                )
            )
        if add:
            copies.append(begin(before[0].at[part], held.at[part]))
        parts.append(copies)
    later = []
    for slot, block in enumerate(ahead):
        later += fetch(block, ahead_ref, slot)
    for copy in ready:
        copy.wait()
    leaving = []
    for part in range(2):
        for copy in parts[part]:
            copy.wait()
        first, last = spans[part]
        for half in range(2):
            cols = slice(half * ROWS, (half + 1) * ROWS)
            total = jnp.dot(
                states[:, first * ROWS : last * ROWS],
                stacks[part][:, cols],
                preferred_element_type=F32,
            )
            if add:
                total = total + held[part, :, cols]
            if ahead:
                out_ref[part, :, cols] = total
            else:
                held[part, :, cols] = total
        if not ahead:
            copy = pltpu.make_async_copy(held.at[part], out_ref.at[part], out_sems.at[part])
            copy.start()
            leaving.append(copy)
    for copy in later + leaving:
        copy.wait()


def multiply(hidden, hidden_other, blocks, pieces, place, total=None, ahead=()):
    weights, moves, spans = [], [], []
    for which, part in enumerate(pieces):
        slots = [slot for _, places in part for slot in places]
        first, last = min(slots), max(slots) + 1
        assert sorted(slots) == list(range(first, last))
        spans.append((first, last))
        moves.append([])
        for rows, places in part:
            col = which * HALF if rows.shape[1] > HALF else 0
            for i, slot in enumerate(places):
                moves[-1].append((len(weights), i * ROWS, col, (slot - first) * ROWS))
            weights.append(rows)
    n_h, n_w, n_a = len(blocks), len(weights), len(ahead)
    add = 0 if total is None else 1
    far = pl.BlockSpec(memory_space=pltpu.HBM)
    near = pl.BlockSpec(memory_space=pltpu.VMEM)
    n_sems = 2 * (n_h + n_a) + sum(len(m) for m in moves) + 2 * add
    scratch = [pltpu.VMEM((2 * TOK, n_h * ROWS), BF16)]
    scratch += [pltpu.VMEM(((last - first) * ROWS, HALF), BF16) for first, last in spans]
    scratch += [
        pltpu.VMEM((2, 2 * TOK, HALF), F32),
        pltpu.SemaphoreType.DMA((2,)),
        pltpu.SemaphoreType.DMA((n_sems,)),
    ]
    out_shape = [jax.ShapeDtypeStruct((2, 2 * TOK, HALF), F32)]
    if ahead:
        out_shape.append(jax.ShapeDtypeStruct((2 * TOK, n_a * ROWS), BF16))
    return pl.pallas_call(
        functools.partial(multiply_kernel, blocks, moves, spans, n_w, add, ahead),
        out_shape=out_shape,
        in_specs=[pl.BlockSpec(memory_space=pltpu.SMEM)] + [far] * (2 + n_w + add),
        out_specs=[near] * 2 if ahead else [far],
        scratch_shapes=scratch,
        cost_estimate=NO_COST,
        compiler_params=pltpu.CompilerParams(vmem_limit_bytes=(48 if ahead else 60) * 2**20),
    )(place, hidden, hidden_other, *weights, *([total] * add))


def finish_kernel(
    states_ref, total_ref, near_ref, far_ref, val_in_ref,
    key_ref, val_ref, key_swap_ref, val_swap_ref
):
    uses = ((near_ref, 0, 0), (far_ref, 0, 1), (val_in_ref, 1, 0))
    outs = ((key_ref, key_swap_ref), (val_ref, val_swap_ref))
    for part in range(2):
        for half in range(2):
            cols = slice(half * ROWS, (half + 1) * ROWS)
            total = total_ref[part, :, cols]
            for ref, where, slot in uses:
                if where == part:
                    total = total + jnp.dot(
                        states_ref[:, slot * ROWS : (slot + 1) * ROWS],
                        ref[:, cols],
                        preferred_element_type=F32,
                    )
            mine_ref, swap_ref = outs[part]
            mine_ref[:, cols] = total[:TOK]
            swap_ref[:, cols] = total[TOK:].astype(swap_ref.dtype)


def finish(states, total, keys_near, keys_far, vals):
    near = pl.BlockSpec(memory_space=pltpu.VMEM)
    return pl.pallas_call(
        finish_kernel,
        out_shape=[
            jax.ShapeDtypeStruct((TOK, HALF), F32),
            jax.ShapeDtypeStruct((TOK, HALF), F32),
            jax.ShapeDtypeStruct((TOK, HALF), F32),
            jax.ShapeDtypeStruct((TOK, HALF), BF16),
        ],
        in_specs=[near] * 5,
        out_specs=[near] * 4,
        cost_estimate=NO_COST,
        compiler_params=pltpu.CompilerParams(vmem_limit_bytes=6 * 2**20),
    )(states, total, keys_near, keys_far, vals)


def rope(head, cosine, sine):
    return head * cosine + pltpu.roll(head, HEAD // 2, 1) * sine


def rotate_kernel(query_ref, cos_ref, sin_ref, out_ref):
    for h in range(GROUP_HEADS):
        cols = slice(h * HEAD, (h + 1) * HEAD)
        out_ref[:, cols] = rope(
            query_ref[:, cols].astype(F32), cos_ref[...], sin_ref[...]
        ).astype(BF16)


def rotate_queries(queries, cosine, sine):
    width = GROUP_HEADS * HEAD
    spec = pl.BlockSpec((TOK, width), lambda h: (0, h))
    table = pl.BlockSpec((TOK, HEAD), lambda h: (0, 0))
    return pl.pallas_call(
        rotate_kernel,
        out_shape=jax.ShapeDtypeStruct(queries.shape, BF16),
        grid=(KV_HEADS,),
        in_specs=[spec, table, table],
        out_specs=spec,
        cost_estimate=NO_COST,
        compiler_params=pltpu.CompilerParams(vmem_limit_bytes=6 * 2**20),
    )(queries, cosine, sine)


def attend_kernel(
    query_ref, key_ref, key_add_ref, val_ref, val_add_ref, cos_ref, sin_ref, bias_ref, out_ref
):
    keys = rope(key_ref[...] + key_add_ref[...], cos_ref[...], sin_ref[...]).astype(BF16)
    vals = (val_ref[...] + val_add_ref[...].astype(F32)).astype(BF16)
    vals = jnp.concatenate([vals, jnp.ones((TOK, HEAD), BF16)], axis=1)
    factor = math.log2(math.e) / math.sqrt(HEAD)
    part = TOK // 2
    for r in range(2):
        rows = slice(r * part, (r + 1) * part)
        seen = (r + 1) * part
        heads = [query_ref[rows, h * HEAD : (h + 1) * HEAD] for h in range(GROUP_HEADS)]
        scores = lax.dot_general(
            jnp.concatenate(heads, axis=0),
            keys[:seen],
            (((1,), (1,)), ((), ())),
            preferred_element_type=F32,
        )
        scores = scores.reshape(GROUP_HEADS, part, seen) + bias_ref[rows, :seen][None]
        peak = jnp.max(scores, axis=2, keepdims=True)
        weights = jnp.exp2((scores - peak) * factor).astype(BF16)
        both = jnp.dot(
            weights.reshape(GROUP_HEADS * part, seen),
            vals[:seen],
            preferred_element_type=F32,
        )
        context = (both[:, :HEAD] / both[:, HEAD:]).astype(BF16)
        for h in range(GROUP_HEADS):
            out_ref[rows, h * HEAD : (h + 1) * HEAD] = context[h * part : (h + 1) * part]


def attend(rotated, keys, keys_add, vals, vals_add, cosine, sine, bias):
    width = GROUP_HEADS * HEAD
    wide = pl.BlockSpec((TOK, width), lambda h: (0, h))
    one = pl.BlockSpec((TOK, HEAD), lambda h: (0, h))
    table = pl.BlockSpec((TOK, HEAD), lambda h: (0, 0))
    square = pl.BlockSpec((TOK, TOK), lambda h: (0, 0))
    return pl.pallas_call(
        attend_kernel,
        out_shape=jax.ShapeDtypeStruct(rotated.shape, BF16),
        grid=(KV_HEADS,),
        in_specs=[wide, one, one, one, one, table, table, square],
        out_specs=wide,
        cost_estimate=NO_COST,
        compiler_params=pltpu.CompilerParams(vmem_limit_bytes=12 * 2**20),
    )(rotated, keys, keys_add, vals, vals_add, cosine, sine, bias)


def tables(token_row):
    token = jnp.arange(TOK, dtype=jnp.int32)
    started = (token_row == BOS)[None, :] & (token[None, :] <= token[:, None])
    latest = jnp.max(jnp.where(started, token[None, :], 0), axis=1)
    positions = (token - latest).astype(F32)
    steps = jnp.arange(HEAD // 2, dtype=F32)
    inverse = rope_base ** (-2.0 * steps / HEAD)
    angles = positions[:, None] * inverse[None, :]
    cosine, sine = jnp.cos(angles), jnp.sin(angles)
    allowed = (token[None, :] <= token[:, None]) & (token[None, :] >= latest[:, None])
    bias = jnp.where(allowed, 0.0, -1e30).astype(F32)
    return (
        jnp.concatenate([cosine, cosine], axis=1),
        jnp.concatenate([-sine, sine], axis=1),
        bias,
    )


def top_bit(number):
    return 31 - lax.clz(jnp.maximum(number, 1))


def power(exponent):
    return lax.shift_left(jnp.full(exponent.shape, 1, jnp.int32), exponent).astype(F32)


def encode_kernel(base_ref, weight_ref, out_ref):
    lanes = lax.broadcasted_iota(jnp.int32, (base_ref.shape[0], HEAD), 1)
    for j in range(base_ref.shape[1] // HEAD):
        cols = slice(j * HEAD, (j + 1) * HEAD)
        delta = base_ref[:, cols] - weight_ref[:, cols].astype(F32)
        size = jnp.abs(delta)
        peak = size
        for reach in (1, 2, 4, 8, 16):
            peak = jnp.maximum(peak, pltpu.roll(peak, reach, 1))
        peak = jnp.take_along_axis(peak, lanes | (BLOCK - 1), axis=1)
        block = top_bit((peak * 2.0**30).astype(jnp.int32))
        value = (size * (power(30 - block) * 2.0**29)).astype(jnp.int32)
        step = jnp.maximum(top_bit(value), 15) - 3
        half = lax.shift_left(jnp.full(step.shape, 1, jnp.int32), step - 1)
        counted = lax.shift_right_logical(value + half, step)
        value = jnp.minimum(lax.shift_left(counted, step), 448 * 2**21)
        code = value.astype(F32) * (power(block) * 2.0**-59)
        out_ref[:, cols] = jnp.where(delta < 0, -code, code).astype(BF16)


def encode(base, weights):
    rows, width = base.shape
    tall = rows // 2
    spec = pl.BlockSpec((tall, width), lambda i: (i, 0))
    return pl.pallas_call(
        encode_kernel,
        out_shape=jax.ShapeDtypeStruct(base.shape, BF16),
        grid=(2,),
        in_specs=[spec, spec],
        out_specs=spec,
        cost_estimate=NO_COST,
        compiler_params=pltpu.CompilerParams(vmem_limit_bytes=56 * 2**20),
    )(base, weights)


def body(
    hidden_states, queries, token_ids, local_weights, outer_base, momentum, outer_rates, frag_index
):
    own = local_weights[0]
    place = lax.axis_index("fsdp")
    z, y, core = place // (Y_HI * CORES), (place // CORES) % Y_HI, place % CORES

    place = jnp.stack([z, y, core]).astype(jnp.int32)

    groups = lax.axis_size("rep")

    def along_x(pick):
        return [(i, i // X * X + pick(i % X)) for i in range(groups)]

    def add(mine, theirs):
        return (mine.astype(F32) + theirs.astype(F32)).astype(BF16)

    hidden_other = send(hidden_states, SWAP)
    up, down = [send(own, UP)], [send(own, DOWN)]
    keys_across = send(own[:, :HALF], ACROSS)
    across = [send(own[:, HALF:], ACROSS)]

    def halves(*blocks):
        return collect(blocks, [[(i, HALF) for i in range(len(blocks))]])[0]

    hidden_other, own_ = tie(hidden_other, own)
    decoded = encode(outer_base, own_)
    up[0], down[0], keys_across, decoded, queries, token_ids = tie(
        up[0], down[0], keys_across, decoded, queries, token_ids
    )
    up.append(send(up[0], UP))
    down.append(send(down[0], DOWN))
    far_up = [send(keys_across, UP)]
    rest = lax.ppermute(decoded, "rep", along_x(lambda x: x ^ 1))
    across.append(send(halves(up[0], down[0]), ACROSS))

    cosine, sine, bias = tables(token_ids)
    table = jnp.arange(outer_rates.shape[0], dtype=jnp.int32)
    rate = jnp.sum(jnp.where(table == frag_index[0], outer_rates, 0.0))
    rotated = rotate_queries(queries, cosine, sine)

    (total,) = multiply(
        hidden_states,
        hidden_other,
        [(0, 0), (0, 1), (-1, 0), (1, 0)],
        [
            [(own, (0,)), (keys_across, (1,)), (up[0], (2,)), (down[0], (3,))],
            [(own, (0,)), (across[0], (1,)), (up[0], (2,)), (down[0], (3,))],
        ],
        place,
    )
    up[1], down[1], rotated, total, rate = tie(up[1], down[1], rotated, total, rate)
    up.append(send(up[1], UP))
    down.append(send(down[1], DOWN))
    up[1], down[1], far_up[0], across[1], rest, keys_across = tie(
        up[1], down[1], far_up[0], across[1], rest, keys_across
    )
    far_up.append(send(far_up[0], UP))
    far_down = [send(keys_across, DOWN)]
    across.append(send(halves(up[1], down[1]), ACROSS))
    part = add(decoded, rest)
    (total,) = multiply(
        hidden_states,
        hidden_other,
        [(-1, 1), (-2, 0), (2, 0), (1, 1)],
        [
            [(far_up[0], (0,)), (up[1], (1,)), (down[1], (2,))],
            [(across[1], (0, 3)), (up[1], (1,)), (down[1], (2,))],
        ],
        place,
        total,
    )
    up[2], down[2], total, part = tie(up[2], down[2], total, part)
    val_last, key_last, vals = collect(
        (up[2], down[2]), [[(0, HALF)], [(1, 0)], [(0, HALF), (1, HALF)]]
    )
    val_last = send(val_last, UP)
    key_last = send(key_last, DOWN)
    up[2], down[2], far_up[1], far_down[0], across[2], vals = tie(
        up[2], down[2], far_up[1], far_down[0], across[2], vals
    )
    far_up.append(send(far_up[1], UP))
    far_down.append(send(far_down[0], DOWN))
    across.append(send(vals, ACROSS))

    (total,) = multiply(
        hidden_states,
        hidden_other,
        [(1, 1), (-2, 1), (-3, 0), (3, 0), (2, 1)],
        [
            [(far_down[0], (0,)), (far_up[1], (1,)), (up[2], (2,)), (down[2], (3,))],
            [(across[2], (1, 4)), (up[2], (2,)), (down[2], (3,))],
        ],
        place,
        total,
    )
    val_last, key_last, total = tie(val_last, key_last, total)
    across.append(send(val_last, ACROSS))
    val_last, key_last, far_up[2], far_down[1], across[3], part = tie(
        val_last, key_last, far_up[2], far_down[1], across[3], part
    )
    far_up.append(send(far_up[2], UP))
    far_down.append(send(far_down[1], DOWN))
    rest = lax.ppermute(part, "rep", along_x(lambda x: X - 1 - x))
    total, states = multiply(
        hidden_states,
        hidden_other,
        [(2, 1), (-3, 1), (4, 0), (3, 1)],
        [
            [(far_down[1], (0,)), (far_up[2], (1,)), (key_last, (2,))],
            [(across[3], (1, 3)), (val_last, (2,))],
        ],
        place,
        total,
        ahead=((4, 1), (3, 1)),
    )
    key_own, val_own, key_swap, val_swap = finish(
        states, total, far_up[3], far_down[2], across[4]
    )
    rest, key_own = tie(rest, key_own)
    part = add(part, rest)
    rest = lax.ppermute(part, "rep", [(i, (i + X) % groups) for i in range(groups)])
    key_add, val_add = send(key_swap, SWAP), send(val_swap, SWAP)
    context = attend(rotated, key_own, key_add, val_own, val_add, cosine, sine, bias)
    context, rest = tie(context, rest)
    outer_grad = (part.astype(F32) + rest.astype(F32)) / groups
    new_momentum = momentum_coef * momentum + outer_grad
    new_base = outer_base - rate * (outer_grad + momentum_coef * new_momentum)
    return (context, new_base, new_momentum)


def solution(mesh):
    placed = (
        P(("rep", "fsdp"), None),
        P(("rep", "fsdp"), None),
        P(("rep", "fsdp")),
        P("rep", "fsdp", None),
        P("fsdp", None),
        P("fsdp", None),
        P(),
        P(),
    )
    return jax.shard_map(
        body,
        mesh=mesh,
        in_specs=placed,
        out_specs=(P(("rep", "fsdp"), None), P("fsdp", None), P("fsdp", None)),
        check_vma=False,
    )
```
